512 devices in a mesh: col: 512 (over x, z, y, core).
Axes of the slice: x: 4, y: 4, z: 16, core: 2. Of those that a mesh axis runs over, the one named last changes fastest.
Arguments:
- final_adjoint: float32 [7, 50, 65536], P(None, None, 'col'), may hold values from -6 to 6
- states: float32 [3, 7, 50, 65536], P(None, None, None, 'col'), may hold values from 0.05 to 3
- implicit: float32 [50, 50, 65536], P(None, None, 'col'), may hold values from -0.6 to 1
- wet_levels: int32 [65536], P('col'), may hold values from 12 to 50
- tile_rows: int32 [15360], P('col'), may hold values from 0 to 25599, as said below
- tile_cols: int32 [15360], P('col'), may hold values from 0 to 25599, as said below
- tiles: bfloat16 [15360, 128, 128], P('col'), may hold values from -0.3984375 to 0.3984375
- tile_count: int32 [512], P('col'), may hold values from 5 to 30, as said below
Outputs:
- initial_adjoint: float32 [7, 50, 65536], P(None, None, 'col')
The draws below stay inside these ranges and needn't reach their ends.
Inputs may be any that keep to these rules, and one draw needn't show every extreme that they name: `tile_rows`: a tile slot of device d names a row block of device d. `tile_cols`: a tile's column block lies on a device at most 2 away from the device of its row block. Slots from tile_count on are not part of the matrix; some device fills all 30 slots.
All inputs are finite; a program needn't handle non-finite values.
Results may differ from the reference program's by a relative error of at most 0.0003.
Values sent between devices are 32-bit elements; how exact they have to be, the bound alone decides.
No kernel may reach another device: no remote copies, remote signals or barrier semaphores. Data moves between devices by JAX's collectives and lax.ppermute only.
A program may use at most 64 MiB of HBM per device.

```python
import math
import jax
import jax.numpy as jnp
from jax import lax

TRC = 7
LEV = 50
COL_DEV = 128
STEPS = 3
REACH = 2
BLOCKS_DEV = 50
TILE_MAX = 30
BLOCKS = 25600
COLUMNS = 65536
N_COL = 512


def draw_implicit(key, part):
    key = jax.random.fold_in(key, 5)
    first, second = jax.random.split(key)
    diagonal = 0.6 + 0.3 * jax.random.uniform(first, (1, LEV, COLUMNS), jnp.float32)
    spread = jnp.clip(0.35 * jax.random.normal(second, (LEV, LEV, COLUMNS), jnp.float32), -0.6, 0.6) / LEV ** 0.5
    upper = jax.lax.broadcasted_iota(jnp.int32, (LEV, LEV, COLUMNS), 0)
    lower = jax.lax.broadcasted_iota(jnp.int32, (LEV, LEV, COLUMNS), 1)
    return jnp.where(upper == lower, diagonal, spread).astype(jnp.float32)


def draw_wet_levels(key, part):
    key = jax.random.fold_in(key, 7)
    levels = jax.random.randint(key, (COLUMNS,), LEV // 4, LEV + 1)
    return levels.at[0].set(LEV).at[1].set(LEV // 4).astype(jnp.int32)


def draw_tile_rows(key, part):
    key = jax.random.fold_in(key, 11)
    owner = jnp.arange(TILE_MAX * N_COL, dtype=jnp.int32) // TILE_MAX
    local = jax.random.randint(key, (TILE_MAX * N_COL,), 0, BLOCKS_DEV)
    rows = owner * BLOCKS_DEV + local
    return rows.at[0].set(0).at[TILE_MAX * N_COL - 1].set(BLOCKS - 1).astype(jnp.int32)


def draw_tile_cols(key, part):
    key = jax.random.fold_in(key, 13)
    first, second = jax.random.split(key)
    position = jnp.arange(TILE_MAX * N_COL, dtype=jnp.int32)
    owner = position // TILE_MAX
    within = position % TILE_MAX
    drawn = jax.random.randint(first, (TILE_MAX * N_COL,), -REACH, REACH + 1)
    offset = jnp.where(within < 2 * REACH + 1, within - REACH, drawn)
    target = jnp.clip(owner + offset, 0, N_COL - 1)
    local = jax.random.randint(second, (TILE_MAX * N_COL,), 0, BLOCKS_DEV)
    cols = target * BLOCKS_DEV + local
    return cols.at[0].set(0).at[TILE_MAX * N_COL - 1].set(BLOCKS - 1).astype(jnp.int32)


def draw_tile_count(key, part):
    key = jax.random.fold_in(key, 17)
    first, second, third = jax.random.split(key, 3)
    lowest = 2 * REACH + 1
    base = jax.random.randint(first, (N_COL,), lowest, TILE_MAX)
    filled = jax.random.randint(second, (N_COL,), 0, 8) == 0
    chosen = jax.random.randint(third, (), 0, N_COL)
    filled = filled | (jnp.arange(N_COL, dtype=jnp.int32) == chosen)
    return jnp.where(filled, TILE_MAX, base).astype(jnp.int32)


def level_of(stream_key, extent, pieces, smallest, top_value):
    gain, own = 1.0, jax.random.fold_in(stream_key, 6)
    for dim, blocks in pieces:
        heights = jnp.exp(jax.random.uniform(jax.random.fold_in(own, dim), (blocks,), jnp.float32, smallest / len(pieces), top_value / len(pieces)))
        gain = gain * jnp.repeat(heights, extent[dim] // blocks).reshape([-1 if axis == dim else 1 for axis in range(len(extent))])
    return gain


def noise(stream_key, extent, deviation, limit, cuts=(), held_as=jnp.bfloat16):
    array = jax.random.normal(stream_key, extent, jnp.float32) * deviation
    if len(cuts) > 0:
        array = level_of(stream_key, extent, cuts, -0.22, 0.18) * array
    return jnp.clip(array, min=-limit, max=limit).astype(held_as)


def setup_inputs(seed: int = 0) -> dict:
    keys = jax.random.split(jax.random.key(seed), 9)
    return {
        "final_adjoint": noise(keys[0], (TRC, LEV, COLUMNS), 1.0, 6.0, ((2, 512),), jnp.float32),
        "states": jnp.clip(jnp.exp(math.log(3.0) - 4.0943445 * jax.random.uniform(keys[1], (STEPS, TRC, LEV, COLUMNS), jnp.float32) ** level_of(keys[1], (STEPS, TRC, LEV, COLUMNS), ((3, 512),), -0.2, 0.2)), 0.05, 3.0),
        "implicit": draw_implicit(jax.random.fold_in(keys[8], 71), 0),
        "wet_levels": draw_wet_levels(jax.random.fold_in(keys[8], 71), 0),
        "tile_rows": draw_tile_rows(jax.random.fold_in(keys[8], 71), 0),
        "tile_cols": draw_tile_cols(jax.random.fold_in(keys[8], 71), 0),
        "tiles": noise(keys[6], (TILE_MAX * N_COL, 128, 128), 0.05, 0.3984375, ((0, 512),)),
        "tile_count": draw_tile_count(jax.random.fold_in(keys[8], 71), 0),
    }


def sources(state, light_factor):
    phosphate, dissolved, oxygen, plankton, grazers, detritus, nitrate = [state[i] for i in range(7)]
    growth = 1.2 * light_factor * plankton * phosphate / (0.03 + phosphate) * nitrate / (0.5 + nitrate)
    grazing = 1.9 * grazers * plankton * plankton / (0.1 + plankton * plankton)
    mortality = 0.03 * plankton * plankton
    remineral = 0.05 * detritus * oxygen / (1.0 + oxygen)
    dop_decay = 0.17 * dissolved
    grazer_loss = 0.05 * grazers * grazers
    return jnp.stack([-growth + remineral + dop_decay + 0.3 * grazing, 0.1 * growth + 0.1 * mortality - dop_decay, 1.2 * (growth - remineral - dop_decay), growth - grazing - mortality, 0.7 * grazing - grazer_loss, grazer_loss + 0.9 * mortality - remineral, 1.6 * (remineral + dop_decay - growth)])

def to_blocks(field):
    shaped = field.reshape(TRC, LEV, N_COL, COL_DEV // 128, 128)
    return jnp.transpose(shaped, (2, 1, 3, 0, 4)).reshape(BLOCKS, TRC, 128)

def from_blocks(blocked):
    shaped = blocked.reshape(N_COL, LEV, COL_DEV // 128, TRC, 128)
    return jnp.transpose(shaped, (3, 1, 0, 2, 4)).reshape(TRC, LEV, COLUMNS)

def reference(final_adjoint, states, implicit, wet_levels, tile_rows, tile_cols, tiles, tile_count):
    levels = lax.broadcasted_iota(jnp.int32, (LEV, COLUMNS), 0)
    wet_mask = (levels < wet_levels[None, :]).astype(jnp.float32)
    light_factor = jnp.exp(-0.2 * lax.broadcasted_iota(jnp.int32, (LEV, 1), 0).astype(jnp.float32))
    row_table = tile_rows.reshape(N_COL, TILE_MAX)
    tile_table = tiles.reshape(N_COL, TILE_MAX, 128, 128)
    active = (lax.broadcasted_iota(jnp.int32, (N_COL, TILE_MAX), 1) < tile_count[:, None]).astype(jnp.float32)
    adjoint = final_adjoint
    for section in range(STEPS - 1, -1, -1):
        carried = jnp.einsum('klc,tkc->tlc', implicit, adjoint, precision=lax.Precision.HIGHEST) * wet_mask
        blocked = to_blocks(carried)

        def device_terms(packed):
            row_ids, matrices, weights = packed
            picked = blocked[row_ids]
            terms = jnp.einsum('sci,sij->scj', picked, matrices.astype(jnp.float32), precision=lax.Precision.HIGHEST)
            return terms * weights[:, None, None]
        contributions = lax.map(device_terms, (row_table, tile_table, active))
        summed = jax.ops.segment_sum(contributions.reshape(-1, TRC, 128), tile_cols, num_segments=BLOCKS)
        transport = from_blocks(summed)
        unused, pull_back = jax.vjp(lambda state: sources(state, light_factor), states[section])
        biology = pull_back(carried)[0]
        adjoint = wet_mask * (carried + transport + 0.5 * biology)
    return adjoint
```

```python
import functools
import jax
import jax.numpy as jnp
from jax import lax
from jax.experimental import pallas as pl
from jax.experimental.pallas import tpu as pltpu
from jax.sharding import PartitionSpec as P

STEPS = 3
TRC = 7
LEV = 50
PAD = 56
SLOTS = 30
REACH = 2
KEYS = 2 * REACH + 1
time_step = 0.5
BLK, ROW, SLOT, START = 0, 32, 64, 96


def pull_back(states, carried, light):
    phosphate, _, oxygen, plankton, grazers, detritus, nitrate = states
    c_pho, c_dis, c_oxy, c_pla, c_gra, c_det, c_nit = carried
    rp = 1.0 / (0.03 + phosphate)
    rn = 1.0 / (0.5 + nitrate)
    ro = 1.0 / (1.0 + oxygen)
    p2 = plankton * plankton
    rg = 1.0 / (0.1 + p2)
    mix = c_pho - 1.2 * c_oxy + 1.6 * c_nit
    a_growth = 0.1 * c_dis + c_pla - mix
    a_grazing = 0.3 * c_pho - c_pla + 0.7 * c_gra
    a_mortality = 0.1 * c_dis - c_pla + 0.9 * c_det
    a_remineral = mix - c_det
    a_decay = mix - c_dis
    a_loss = c_det - c_gra
    fp = phosphate * rp
    fn = nitrate * rn
    lg = (1.2 * light) * a_growth
    lgp = lg * plankton
    d_pho = lgp * fn * (0.03 * rp * rp)
    d_nit = lgp * fp * (0.5 * rn * rn)
    hol = p2 * rg
    ag = 1.9 * a_grazing
    d_pla = lg * fp * fn + ag * grazers * (0.2 * plankton * rg * rg) + 0.06 * plankton * a_mortality
    d_gra = ag * hol + 0.1 * grazers * a_loss
    ar = 0.05 * a_remineral
    d_det = ar * oxygen * ro
    d_oxy = ar * detritus * (ro * ro)
    d_dis = 0.17 * a_decay
    return [d_pho, d_dis, d_oxy, d_pla, d_gra, d_det, d_nit]


def advance(adj_ref, implicit_ref, states_ref, wet, base_ref, planes):
    level_ids = lax.broadcasted_iota(jnp.int32, (LEV, 128), 0)
    mask = (level_ids < wet).astype(jnp.float32)
    light = jnp.exp(-0.2 * level_ids.astype(jnp.float32))

    def term(k, acc):
        m = implicit_ref[k]
        return tuple(acc[t] + m * adj_ref[t, pl.ds(k, 1), :] for t in range(TRC))

    acc = tuple(jnp.zeros((LEV, 128), jnp.float32) for _ in range(TRC))
    acc = lax.fori_loop(0, LEV, term, acc, unroll=5)
    carried = [a * mask for a in acc]
    for t in range(TRC):
        planes[pl.ds(t, LEV, stride=8), :] = carried[t]
    bio = pull_back([states_ref[t] for t in range(TRC)], carried, light)
    for t in range(TRC):
        base_ref[t] = carried[t] + time_step * bio[t]


def make_terms(planes, tiles_ref, slot_of, row_of, out_ref):
    for p in range(SLOTS):
        row = pl.multiple_of(row_of(p) * 8, 8)
        picked = planes[pl.ds(row, 8), :]
        hi = picked.astype(jnp.bfloat16)
        lo = (picked - hi.astype(jnp.float32)).astype(jnp.bfloat16)
        both = jnp.concatenate([hi, lo], axis=0)
        prod = jnp.dot(both, tiles_ref[slot_of(p)], preferred_element_type=jnp.float32)
        out_ref[p] = prod[:8] + prod[8:]


def first_kernel(rows, cols, count, wet_ref, final_ref, implicit_ref, states_ref, tiles_ref,
                 out_ref, base_ref, planes, order, starts):
    me = lax.axis_index("col")
    live = count[0]
    origin = (me - REACH) * LEV

    def key_of(s):
        r = cols[s] - origin
        return sum((r >= LEV * j).astype(jnp.int32) for j in range(1, KEYS)), r

    for j in range(8):
        starts[j] = 0

    def tally(s, carry):
        key, _ = key_of(s)
        starts[key + 1] = starts[key + 1] + 1
        return carry

    lax.fori_loop(0, live, tally, 0)
    for j in range(1, 7):
        starts[j] = starts[j] + starts[j - 1]
    lane = lax.broadcasted_iota(jnp.int32, (1, 128), 1)
    info = jnp.zeros((1, 128), jnp.int32)
    for j in range(KEYS + 1):
        info = jnp.where(lane == START + j, starts[j], info)
    for p in range(3 * 32):
        order[p] = 0

    def place(s, carry):
        key, r = key_of(s)
        p = starts[key]
        starts[key] = p + 1
        order[BLK + p] = r - LEV * key
        order[ROW + p] = rows[s] - me * LEV
        order[SLOT + p] = s
        return carry

    lax.fori_loop(0, live, place, 0)
    for p in range(SLOTS):
        for base in (BLK, ROW, SLOT):
            info = jnp.where(lane == base + p, order[base + p], info)

    planes[...] = jnp.zeros_like(planes)
    advance(final_ref, implicit_ref, states_ref, wet_ref[...], base_ref, planes)
    make_terms(planes, tiles_ref, lambda p: order[SLOT + p], lambda p: order[ROW + p], out_ref)
    out_ref[0, 7:8, :] = info.astype(jnp.float32)


def receive(got_ref, info_v, info_s, planes, sem):
    me = lax.axis_index("col")
    core = lax.rem(me, 2)
    chip = lax.div(me, 2)
    odd = lax.rem(chip, 2)
    even_chip = chip + 1 - 2 * odd
    odd_chip = chip - 1 + 2 * odd
    places = []
    for k in range(2):
        places.append((2 * odd + k, 2 * chip + k))
        places.append((2 * (1 - odd) + k, 2 * even_chip + k))
        places.append((4 + 2 * odd + k, 2 * odd_chip + k))
    for i, (chunk, _) in enumerate(places):
        info_v[i : i + 1, :] = got_ref[chunk * SLOTS, 7:8, :].astype(jnp.int32)
    copy = pltpu.make_async_copy(info_v, info_s, sem)
    copy.start()
    planes[...] = jnp.zeros_like(planes)
    copy.wait()
    for i, (chunk, src) in enumerate(places):
        key = me - src + REACH
        inside = (key >= 0) & (key < KEYS)
        safe = jnp.clip(key, 0, KEYS - 1)
        begin = info_s[i, START + safe]
        end = jnp.where(inside, info_s[i, START + safe + 1], begin)

        def add(p, carry, i=i, chunk=chunk):
            at = pl.multiple_of(info_s[i, BLK + p] * 8, 8)
            planes[pl.ds(at, 8), :] = planes[pl.ds(at, 8), :] + got_ref[chunk * SLOTS + p]
            return carry

        lax.fori_loop(begin, end, add, 0)
    return jnp.where(core == 0, 0, 3)


def gather_adjoint(planes, base_ref, wet, out_ref):
    level_ids = lax.broadcasted_iota(jnp.int32, (LEV, 128), 0)
    mask = (level_ids < wet).astype(jnp.float32)
    for t in range(TRC):
        out_ref[t] = mask * (base_ref[t] + planes[pl.ds(t, LEV, stride=8), :])


def next_kernel(got_ref, wet_ref, base_in, implicit_ref, states_ref, tiles_ref, out_ref, base_ref,
                planes, adj, info_v, info_s, sem):
    own = receive(got_ref, info_v, info_s, planes, sem)
    gather_adjoint(planes, base_in, wet_ref[...], adj)
    planes[...] = jnp.zeros_like(planes)
    advance(adj, implicit_ref, states_ref, wet_ref[...], base_ref, planes)
    make_terms(planes, tiles_ref, lambda p: info_s[own, SLOT + p], lambda p: info_s[own, ROW + p], out_ref)
    out_ref[0, 7:8, :] = info_v[pl.ds(own, 1), :].astype(jnp.float32)


def last_kernel(got_ref, wet_ref, base_in, out_ref, planes, info_v, info_s, sem):
    receive(got_ref, info_v, info_s, planes, sem)
    gather_adjoint(planes, base_in, wet_ref[...], out_ref)


VMEM = pl.BlockSpec(memory_space=pltpu.VMEM)
SMEM = pl.BlockSpec(memory_space=pltpu.SMEM)
f32 = jnp.float32
PARAMS = pltpu.CompilerParams(vmem_limit_bytes=24 * 1024 * 1024)


def shards(final_adjoint, states, implicit, wet_levels, tile_rows, tile_cols, tiles, tile_count):
    devices = lax.axis_size("col")
    inside = [[2 * c, 2 * c + 1] for c in range(devices // 2)]
    across = [[2 * c, 2 * c + 2] for c in range(0, devices // 2, 2)]
    across += [[2 * c + 1, (2 * c + 3) % devices] for c in range(1, devices // 2, 2)]
    wet = wet_levels.reshape(1, 128)
    slots = jax.ShapeDtypeStruct((SLOTS, 8, 128), f32)
    field = jax.ShapeDtypeStruct((TRC, LEV, 128), f32)
    planes = pltpu.VMEM((PAD * 8, 128), f32)
    infos = [pltpu.VMEM((8, 128), jnp.int32), pltpu.SMEM((8, 128), jnp.int32), pltpu.SemaphoreType.DMA]

    def exchange(terms):
        for groups in (inside, across, inside):
            terms = lax.all_gather(terms, "col", axis_index_groups=groups, tiled=True)
        return terms

    terms, base = pl.pallas_call(
        first_kernel,
        in_specs=[SMEM] * 3 + [VMEM] * 5,
        out_specs=[VMEM] * 2,
        out_shape=[slots, field],
        scratch_shapes=[planes, pltpu.SMEM((96,), jnp.int32), pltpu.SMEM((8,), jnp.int32)],
        compiler_params=PARAMS,
    )(tile_rows, tile_cols, tile_count, wet, final_adjoint, implicit, states[STEPS - 1], tiles)
    for section in range(STEPS - 2, -1, -1):
        got = exchange(terms)
        terms, base = pl.pallas_call(
            next_kernel,
            in_specs=[VMEM] * 6,
            out_specs=[VMEM] * 2,
            out_shape=[slots, field],
            scratch_shapes=[planes, pltpu.VMEM((TRC, LEV, 128), f32)] + infos,
            compiler_params=PARAMS,
        )(got, wet, base, implicit, states[section], tiles)
    got = exchange(terms)
    return pl.pallas_call(
        last_kernel,
        in_specs=[VMEM] * 3,
        out_specs=VMEM,
        out_shape=field,
        scratch_shapes=[planes] + infos,
        compiler_params=PARAMS,
    )(got, wet, base)


def solution(mesh):
    in_specs = (
        P(None, None, "col"),
        P(None, None, None, "col"),
        P(None, None, "col"),
        P("col"),
        P("col"),
        P("col"),
        P("col", None, None),
        P("col"),
    )
    out_specs = P(None, None, "col")
    return jax.shard_map(shards, mesh=mesh, in_specs=in_specs, out_specs=out_specs, check_vma=False)
```

```python
import functools
import jax
import jax.numpy as jnp
from jax import lax
from jax.experimental import pallas as pl
from jax.experimental.pallas import tpu as pltpu
from jax.sharding import PartitionSpec as P

STEPS = 3
TRC = 7
LEV = 50
PAD = 56
SLOTS = 30
REACH = 2
KEYS = 2 * REACH + 1
time_step = 0.5
SPAN = 32
INFO = SLOTS
CHUNK = TRC * SPAN
KEY = 64
NONE = -1000.0


def pull_back(states, carried, light):
    phosphate, _, oxygen, plankton, grazers, detritus, nitrate = states
    c_pho, c_dis, c_oxy, c_pla, c_gra, c_det, c_nit = carried
    rp = 1.0 / (0.03 + phosphate)
    rn = 1.0 / (0.5 + nitrate)
    ro = 1.0 / (1.0 + oxygen)
    p2 = plankton * plankton
    rg = 1.0 / (0.1 + p2)
    mix = c_pho - 1.2 * c_oxy + 1.6 * c_nit
    a_growth = 0.1 * c_dis + c_pla - mix
    a_grazing = 0.3 * c_pho - c_pla + 0.7 * c_gra
    a_mortality = 0.1 * c_dis - c_pla + 0.9 * c_det
    a_remineral = mix - c_det
    a_decay = mix - c_dis
    a_loss = c_det - c_gra
    fp = phosphate * rp
    fn = nitrate * rn
    lg = (1.2 * light) * a_growth
    lgp = lg * plankton
    d_pho = lgp * fn * (0.03 * rp * rp)
    d_nit = lgp * fp * (0.5 * rn * rn)
    hol = p2 * rg
    ag = 1.9 * a_grazing
    d_pla = lg * fp * fn + ag * grazers * (0.2 * plankton * rg * rg) + 0.06 * plankton * a_mortality
    d_gra = ag * hol + 0.1 * grazers * a_loss
    ar = 0.05 * a_remineral
    d_det = ar * oxygen * ro
    d_oxy = ar * detritus * (ro * ro)
    d_dis = 0.17 * a_decay
    return [d_pho, d_dis, d_oxy, d_pla, d_gra, d_det, d_nit]


def wet_mask(wet):
    level_ids = lax.broadcasted_iota(jnp.int32, (LEV, 128), 0)
    return (level_ids < wet).astype(jnp.float32)


def advance(adj_ref, implicit_ref, wet, carried_ref, planes, arrive=None, parts=1):
    def term(k, acc):
        m = implicit_ref[k]
        return tuple(acc[t] + m * adj_ref[t, pl.ds(k, 1), :] for t in range(TRC))

    acc = tuple(jnp.zeros((LEV, 128), jnp.float32) for _ in range(TRC))
    for part in range(parts):
        if arrive is not None:
            arrive(part)
        acc = lax.fori_loop(part * LEV // parts, (part + 1) * LEV // parts, term, acc, unroll=25)
    mask = wet_mask(wet)
    for t in range(TRC):
        carried = acc[t] * mask
        planes[pl.ds(t, LEV, stride=8), :] = carried
        carried_ref[t] = carried


def make_terms(planes, tiles_ref, rows, out_ref):
    origin = lax.axis_index("col") * LEV
    for t in range(TRC):
        out_ref[t * SPAN + 24 : (t + 1) * SPAN, :] = jnp.zeros((8, 128), jnp.float32)
    for p in range(SLOTS):
        row = pl.multiple_of(jnp.clip(rows[p] - origin, 0, LEV - 1) * 8, 8)
        picked = planes[pl.ds(row, 8), :]
        hi = picked.astype(jnp.bfloat16)
        lo = (picked - hi.astype(jnp.float32)).astype(jnp.bfloat16)
        both = jnp.concatenate([hi, lo], axis=0)
        prod = jnp.dot(both, tiles_ref[p], preferred_element_type=jnp.float32)
        out_ref[pl.ds(p, TRC, stride=SPAN), :] = prod[:TRC] + prod[8 : 8 + TRC]


def first_kernel(rows_h, cols_h, count_h, wet_h, final_h, implicit_h, tiles_h,
                 out_ref, carried_ref, wet, implicit, tiles, adj, planes, rows, cols, count, sems):
    used = [0]

    def begin(src, dst):
        copy = pltpu.make_async_copy(src, dst, sems.at[used[0]])
        used[0] += 1
        copy.start()
        return copy

    span = LEV // PARTS
    small = [begin(final_h, adj), begin(wet_h, wet)]
    parts = [begin(implicit_h.at[pl.ds(i * span, span)], implicit.at[pl.ds(i * span, span)]) for i in range(PARTS)]
    small += [begin(cols_h, cols), begin(count_h, count), begin(rows_h, rows)]
    half = SLOTS // 2
    late = [begin(tiles_h.at[pl.ds(i * half, half)], tiles.at[pl.ds(i * half, half)]) for i in range(2)]
    for copy in small[:2]:
        copy.wait()
    advance(adj, implicit, wet[...], carried_ref, planes, lambda i: parts[i].wait(), PARTS)
    for copy in small[2:] + late:
        copy.wait()
    make_terms(planes, tiles, rows, out_ref)
    place = cols[...] - (lax.axis_index("col") - REACH) * LEV
    key = sum((place >= LEV * j).astype(jnp.int32) for j in range(1, KEYS))
    lane = lax.broadcasted_iota(jnp.int32, (1, SLOTS), 1)
    code = jnp.where(lane < count[0], place + (KEY - LEV) * key, -1).astype(jnp.float32)
    out_ref[INFO : INFO + 1, :] = jnp.full((1, 128), -1.0, jnp.float32)
    for i in range(128 // SPAN):
        out_ref[INFO : INFO + 1, i * SPAN : i * SPAN + SLOTS] = code


def origins(split):
    me = lax.axis_index("col")
    chip = lax.div(me, 2)
    odd = lax.rem(chip, 2)
    if split:
        chips = [chip, chip + 1 - 2 * odd, chip - 1 + 2 * odd]
    else:
        even_edge = chip - odd
        odd_edge = chip - 1 + odd
        away = -(2 ** 20)
        chips = [even_edge, even_edge + 1, jnp.where(odd == 1, away, odd_edge), jnp.where(odd == 1, odd_edge + 1, away)]
    return [2 * c + k for c in chips for k in range(2)]


def receive(chunks, split, take):
    me = lax.axis_index("col")
    lane = lax.broadcasted_iota(jnp.int32, (1, 128), 1)
    level = lax.broadcasted_iota(jnp.int32, (64, 128), 0).astype(jnp.float32)
    bases = [jnp.where(src < -REACH, -100, me - src + REACH) * KEY for src in origins(split)]
    per = 128 // SPAN
    marks = []
    for first in range(0, len(chunks), per):
        number = min(per, len(chunks) - first)
        codes = jnp.full((1, 128), NONE, jnp.float32)
        for i in range(number):
            here = (lane >= i * SPAN) & (lane < (i + 1) * SPAN)
            ref, at = chunks[first + i]
            found = ref[at + INFO : at + INFO + 1, :] - bases[first + i].astype(jnp.float32)
            codes = jnp.where(here, found, codes)
        marks.append((level == codes).astype(jnp.float32).astype(jnp.bfloat16)[:, : number * SPAN])
    marks = jnp.concatenate(marks, axis=1)
    for t in range(TRC):
        data = jnp.concatenate([ref[at + t * SPAN : at + (t + 1) * SPAN, :] for ref, at in chunks], axis=0)
        hi = data.astype(jnp.bfloat16)
        lo = (data - hi.astype(jnp.float32)).astype(jnp.bfloat16)
        both = jnp.dot(marks, jnp.concatenate([hi, lo], axis=1), preferred_element_type=jnp.float32)
        take(t, both[:LEV, :128] + both[:LEV, 128:])


def chunks_of(gots):
    return [(ref, at) for ref in gots for at in range(0, ref.shape[0], CHUNK)]


def local_part(carried_ref, states_ref, section, base):
    level_ids = lax.broadcasted_iota(jnp.int32, (LEV, 128), 0)
    light = jnp.exp(-0.2 * level_ids.astype(jnp.float32))
    carried = [carried_ref[t] for t in range(TRC)]
    bio = pull_back([states_ref[section, t] for t in range(TRC)], carried, light)
    for t in range(TRC):
        base[t] = carried[t] + time_step * bio[t]


def adjoint_into(out_ref, gots, wet_ref, base):
    mask = wet_mask(wet_ref[...])

    def take(t, transport):
        out_ref[t] = mask * (base[t] + transport)

    receive(chunks_of(gots), len(gots) == 2, take)


def next_kernel(section, number, *refs):
    gots, refs = refs[:number], refs[number:]
    (rows_h, wet_ref, carried_in, implicit_ref, states_ref, tiles_ref,
     out_ref, carried_ref, base, planes, adj, rows, sem) = refs
    copy = pltpu.make_async_copy(rows_h, rows, sem)
    copy.start()
    local_part(carried_in, states_ref, section + 1, base)
    adjoint_into(adj, gots, wet_ref, base)
    advance(adj, implicit_ref, wet_ref[...], carried_ref, planes)
    copy.wait()
    make_terms(planes, tiles_ref, rows, out_ref)
    me = lax.axis_index("col")
    core = lax.rem(me, 2)
    own = core if number == 2 else 2 * lax.rem(lax.div(me, 2), 2) + core
    out_ref[INFO : INFO + 1, :] = gots[0][pl.ds(own * CHUNK + INFO, 1), :]


def last_kernel(*refs):
    gots, (wet_ref, carried_in, states_ref, out_ref, base) = refs[:-5], refs[-5:]
    local_part(carried_in, states_ref, 0, base)
    adjoint_into(out_ref, gots, wet_ref, base)


VMEM = pl.BlockSpec(memory_space=pltpu.VMEM)
HBM = pl.BlockSpec(memory_space=pltpu.HBM)
f32 = jnp.float32
PARTS = 2
SWAP_STEP = 1
MIB = 1024 * 1024


def shards(final_adjoint, states, implicit, wet_levels, tile_rows, tile_cols, tiles, tile_count):
    devices = lax.axis_size("col")
    inside = [[2 * c, 2 * c + 1] for c in range(devices // 2)]
    across = [[2 * c, 2 * c + 2] for c in range(0, devices // 2, 2)]
    across += [[2 * c + 1, (2 * c + 3) % devices] for c in range(1, devices // 2, 2)]
    swaps = [pair for a, b in across[:-1] for pair in ((a, b), (b, a))]
    slots = jax.ShapeDtypeStruct((CHUNK, 128), f32)
    field = jax.ShapeDtypeStruct((TRC, LEV, 128), f32)
    scratch = pltpu.VMEM((TRC, LEV, 128), f32)
    planes = pltpu.VMEM((PAD * 8, 128), f32)
    rows = pltpu.SMEM((SLOTS,), jnp.int32)
    wet = wet_levels.reshape(1, 128)

    def gather(x, groups):
        return lax.all_gather(x, "col", axis_index_groups=groups, tiled=True)

    def exchange(terms, step):
        own = gather(terms, inside)
        if step == SWAP_STEP:
            return own, gather(lax.ppermute(own, "col", swaps), inside)
        return (gather(gather(own, across), inside),)

    terms, carried = pl.pallas_call(
        first_kernel,
        in_specs=[HBM] * 7,
        out_specs=[VMEM] * 2,
        out_shape=[slots, field],
        scratch_shapes=[
            pltpu.VMEM(wet.shape, wet.dtype),
            pltpu.VMEM(implicit.shape, implicit.dtype),
            pltpu.VMEM(tiles.shape, tiles.dtype),
            scratch,
            planes,
            rows,
            pltpu.VMEM((1, SLOTS), jnp.int32),
            pltpu.SMEM((1,), jnp.int32),
            pltpu.SemaphoreType.DMA((PARTS + 8,)),
        ],
        compiler_params=pltpu.CompilerParams(vmem_limit_bytes=62 * MIB),
        name="first_step",
    )(tile_rows, tile_cols.reshape(1, SLOTS), tile_count, wet, final_adjoint, implicit, tiles)
    for section in range(STEPS - 2, -1, -1):
        gots = exchange(terms, STEPS - 2 - section)
        terms, carried = pl.pallas_call(
            functools.partial(next_kernel, section, len(gots)),
            in_specs=[VMEM] * len(gots) + [HBM] + [VMEM] * 5,
            out_specs=[VMEM] * 2,
            out_shape=[slots, field],
            scratch_shapes=[scratch, planes, scratch, rows, pltpu.SemaphoreType.DMA],
            compiler_params=pltpu.CompilerParams(vmem_limit_bytes=24 * MIB),
            name="next_step",
        )(*gots, tile_rows, wet, carried, implicit, states, tiles)
    gots = exchange(terms, STEPS - 1)
    return pl.pallas_call(
        last_kernel,
        in_specs=[VMEM] * (len(gots) + 3),
        out_specs=VMEM,
        out_shape=field,
        scratch_shapes=[scratch],
        compiler_params=pltpu.CompilerParams(vmem_limit_bytes=24 * MIB),
        name="last_step",
    )(*gots, wet, carried, states)


def solution(mesh):
    in_specs = (
        P(None, None, "col"),
        P(None, None, None, "col"),
        P(None, None, "col"),
        P("col"),
        P("col"),
        P("col"),
        P("col", None, None),
        P("col"),
    )
    out_specs = P(None, None, "col")
    return jax.shard_map(shards, mesh=mesh, in_specs=in_specs, out_specs=out_specs, check_vma=False)
```

```python
import functools
import jax
import jax.numpy as jnp
from jax import lax
from jax.experimental import pallas as pl
from jax.experimental.pallas import tpu as pltpu
from jax.sharding import PartitionSpec as P

STEPS = 3
TRC = 7
LEV = 50
PAD = 56
SLOTS = 30
REACH = 2
KEYS = 2 * REACH + 1
time_step = 0.5
SPAN = 32
INFO = SLOTS
CHUNK = TRC * SPAN
KEY = 64
NONE = -1000.0


def pull_back(states, carried, light):
    phosphate, _, oxygen, plankton, grazers, detritus, nitrate = states
    c_pho, c_dis, c_oxy, c_pla, c_gra, c_det, c_nit = carried
    rp = 1.0 / (0.03 + phosphate)
    rn = 1.0 / (0.5 + nitrate)
    ro = 1.0 / (1.0 + oxygen)
    p2 = plankton * plankton
    rg = 1.0 / (0.1 + p2)
    mix = c_pho - 1.2 * c_oxy + 1.6 * c_nit
    a_growth = 0.1 * c_dis + c_pla - mix
    a_grazing = 0.3 * c_pho - c_pla + 0.7 * c_gra
    a_mortality = 0.1 * c_dis - c_pla + 0.9 * c_det
    a_remineral = mix - c_det
    a_decay = mix - c_dis
    a_loss = c_det - c_gra
    fp = phosphate * rp
    fn = nitrate * rn
    lg = (1.2 * light) * a_growth
    lgp = lg * plankton
    d_pho = lgp * fn * (0.03 * rp * rp)
    d_nit = lgp * fp * (0.5 * rn * rn)
    hol = p2 * rg
    ag = 1.9 * a_grazing
    d_pla = lg * fp * fn + ag * grazers * (0.2 * plankton * rg * rg) + 0.06 * plankton * a_mortality
    d_gra = ag * hol + 0.1 * grazers * a_loss
    ar = 0.05 * a_remineral
    d_det = ar * oxygen * ro
    d_oxy = ar * detritus * (ro * ro)
    d_dis = 0.17 * a_decay
    return [d_pho, d_dis, d_oxy, d_pla, d_gra, d_det, d_nit]


def wet_mask(wet):
    level_ids = lax.broadcasted_iota(jnp.int32, (LEV, 128), 0)
    return (level_ids < wet).astype(jnp.float32)


def product(adj_ref, implicit_ref, arrive=None, parts=1):
    def term(k, acc):
        m = implicit_ref[k]
        return tuple(acc[t] + m * adj_ref[t, pl.ds(k, 1), :] for t in range(TRC))

    acc = tuple(jnp.zeros((LEV, 128), jnp.float32) for _ in range(TRC))
    for part in range(parts):
        if arrive is not None:
            arrive(part)
        acc = lax.fori_loop(part * LEV // parts, (part + 1) * LEV // parts, term, acc, unroll=min(25, LEV // parts))
    return acc


def advance(adj_ref, implicit_ref, wet, carried_ref, planes):
    acc = product(adj_ref, implicit_ref)
    mask = wet_mask(wet)
    for t in range(TRC):
        carried = acc[t] * mask
        planes[pl.ds(t, LEV, stride=8), :] = carried
        carried_ref[t] = carried


def make_terms(planes, tiles_ref, rows, out_ref):
    origin = lax.axis_index("col") * LEV
    for t in range(TRC):
        out_ref[t * SPAN + 24 : (t + 1) * SPAN, :] = jnp.zeros((8, 128), jnp.float32)

    def pick(p):
        row = pl.multiple_of(jnp.clip(rows[p] - origin, 0, LEV - 1) * 8, 8)
        picked = planes[pl.ds(row, 8), :]
        hi = picked.astype(jnp.bfloat16)
        lo = (picked - hi.astype(jnp.float32)).astype(jnp.bfloat16)
        return [hi, lo]

    for p in range(0, SLOTS, 2):
        left = jnp.concatenate(pick(p) + pick(p + 1), axis=0)
        right = jnp.concatenate([tiles_ref[p], tiles_ref[p + 1]], axis=1)
        prod = jnp.dot(left, right, preferred_element_type=jnp.float32)
        out_ref[pl.ds(p, TRC, stride=SPAN), :] = prod[:TRC, :128] + prod[8 : 8 + TRC, :128]
        out_ref[pl.ds(p + 1, TRC, stride=SPAN), :] = prod[16 : 16 + TRC, 128:] + prod[24 : 24 + TRC, 128:]


def first_kernel(final_h, implicit_h, out_ref, implicit, adj, sems):
    span = LEV // PARTS
    copies = [pltpu.make_async_copy(final_h, adj, sems.at[PARTS])]
    for i in range(PARTS):
        part = pl.ds(i * span, span)
        copies.append(pltpu.make_async_copy(implicit_h.at[part], implicit.at[part], sems.at[i]))
    for copy in copies:
        copy.start()
    copies[0].wait()
    acc = product(adj, implicit, lambda i: copies[i + 1].wait(), PARTS)
    for t in range(TRC):
        out_ref[t] = acc[t]


def first_terms(rows_h, cols, count, wet, product_ref, tiles_ref, out_ref, carried_ref, planes, rows, sem):
    copy = pltpu.make_async_copy(rows_h, rows, sem)
    copy.start()
    mask = wet_mask(wet[...])
    for t in range(TRC):
        carried = product_ref[t] * mask
        planes[pl.ds(t, LEV, stride=8), :] = carried
        carried_ref[t] = carried
    place = cols[...] - (lax.axis_index("col") - REACH) * LEV
    key = sum((place >= LEV * j).astype(jnp.int32) for j in range(1, KEYS))
    lane = lax.broadcasted_iota(jnp.int32, (1, SLOTS), 1)
    code = jnp.where(lane < count[...], place + (KEY - LEV) * key, -1).astype(jnp.float32)
    copy.wait()
    make_terms(planes, tiles_ref, rows, out_ref)
    out_ref[INFO : INFO + 1, :] = jnp.full((1, 128), -1.0, jnp.float32)
    for i in range(128 // SPAN):
        out_ref[INFO : INFO + 1, i * SPAN : i * SPAN + SLOTS] = code


def origins(split):
    me = lax.axis_index("col")
    chip = lax.div(me, 2)
    odd = lax.rem(chip, 2)
    if split:
        chips = [chip, chip + 1 - 2 * odd, chip - 1 + 2 * odd]
    else:
        even_edge = chip - odd
        odd_edge = chip - 1 + odd
        away = -(2 ** 20)
        chips = [even_edge, even_edge + 1, jnp.where(odd == 1, away, odd_edge), jnp.where(odd == 1, odd_edge + 1, away)]
    return [2 * c + k for c in chips for k in range(2)]


def receive(chunks, split, take):
    me = lax.axis_index("col")
    lane = lax.broadcasted_iota(jnp.int32, (1, 128), 1)
    level = lax.broadcasted_iota(jnp.int32, (64, 128), 0).astype(jnp.float32)
    bases = [jnp.where(src < -REACH, -100, me - src + REACH) * KEY for src in origins(split)]
    per = 128 // SPAN
    marks = []
    for first in range(0, len(chunks), per):
        number = min(per, len(chunks) - first)
        codes = jnp.full((1, 128), NONE, jnp.float32)
        for i in range(number):
            here = (lane >= i * SPAN) & (lane < (i + 1) * SPAN)
            ref, at = chunks[first + i]
            found = ref[at + INFO : at + INFO + 1, :] - bases[first + i].astype(jnp.float32)
            codes = jnp.where(here, found, codes)
        marks.append((level == codes).astype(jnp.float32).astype(jnp.bfloat16)[:, : number * SPAN])
    marks = jnp.concatenate(marks, axis=1)
    for t in range(TRC):
        data = jnp.concatenate([ref[at + t * SPAN : at + (t + 1) * SPAN, :] for ref, at in chunks], axis=0)
        hi = data.astype(jnp.bfloat16)
        lo = (data - hi.astype(jnp.float32)).astype(jnp.bfloat16)
        both = jnp.dot(marks, jnp.concatenate([hi, lo], axis=1), preferred_element_type=jnp.float32)
        take(t, both[:LEV, :128] + both[:LEV, 128:])


def chunks_of(gots):
    return [(ref, at) for ref in gots for at in range(0, ref.shape[0], CHUNK)]


def local_part(carried_ref, states_ref, section, base):
    level_ids = lax.broadcasted_iota(jnp.int32, (LEV, 128), 0)
    light = jnp.exp(-0.2 * level_ids.astype(jnp.float32))
    carried = [carried_ref[t] for t in range(TRC)]
    bio = pull_back([states_ref[section, t] for t in range(TRC)], carried, light)
    for t in range(TRC):
        base[t] = carried[t] + time_step * bio[t]


def adjoint_into(out_ref, gots, wet_ref, base):
    mask = wet_mask(wet_ref[...])

    def take(t, transport):
        out_ref[t] = mask * (base[t] + transport)

    receive(chunks_of(gots), len(gots) == 2, take)


def next_kernel(section, number, *refs):
    gots, refs = refs[:number], refs[number:]
    (rows_h, wet_ref, carried_in, implicit_ref, states_ref, tiles_ref,
     out_ref, carried_ref, base, planes, adj, rows, sem) = refs
    copy = pltpu.make_async_copy(rows_h, rows, sem)
    copy.start()
    local_part(carried_in, states_ref, section + 1, base)
    adjoint_into(adj, gots, wet_ref, base)
    advance(adj, implicit_ref, wet_ref[...], carried_ref, planes)
    copy.wait()
    make_terms(planes, tiles_ref, rows, out_ref)
    me = lax.axis_index("col")
    core = lax.rem(me, 2)
    own = core if number == 2 else 2 * lax.rem(lax.div(me, 2), 2) + core
    out_ref[INFO : INFO + 1, :] = gots[0][pl.ds(own * CHUNK + INFO, 1), :]


def last_kernel(*refs):
    gots, (wet_ref, carried_in, states_ref, out_ref, base) = refs[:-5], refs[-5:]
    local_part(carried_in, states_ref, 0, base)
    adjoint_into(out_ref, gots, wet_ref, base)


VMEM = pl.BlockSpec(memory_space=pltpu.VMEM)
HBM = pl.BlockSpec(memory_space=pltpu.HBM)
f32 = jnp.float32
PARTS = 5
SWAP_STEP = 1
MIB = 1024 * 1024
FIRST_GRANT = 56255054


def shards(final_adjoint, states, implicit, wet_levels, tile_rows, tile_cols, tiles, tile_count):
    devices = lax.axis_size("col")
    inside = [[2 * c, 2 * c + 1] for c in range(devices // 2)]
    across = [[2 * c, 2 * c + 2] for c in range(0, devices // 2, 2)]
    across += [[2 * c + 1, (2 * c + 3) % devices] for c in range(1, devices // 2, 2)]
    swaps = [pair for a, b in across[:-1] for pair in ((a, b), (b, a))]
    slots = jax.ShapeDtypeStruct((CHUNK, 128), f32)
    field = jax.ShapeDtypeStruct((TRC, LEV, 128), f32)
    scratch = pltpu.VMEM((TRC, LEV, 128), f32)
    planes = pltpu.VMEM((PAD * 8, 128), f32)
    rows = pltpu.SMEM((SLOTS,), jnp.int32)
    wet = wet_levels.reshape(1, 128)

    def gather(x, groups):
        return lax.all_gather(x, "col", axis_index_groups=groups, tiled=True)

    def exchange(terms, step):
        own = gather(terms, inside)
        if step == SWAP_STEP:
            return own, gather(lax.ppermute(own, "col", swaps), inside)
        return (gather(gather(own, across), inside),)

    first = pl.pallas_call(
        first_kernel,
        in_specs=[HBM] * 2,
        out_specs=VMEM,
        out_shape=field,
        scratch_shapes=[pltpu.VMEM(implicit.shape, f32), scratch, pltpu.SemaphoreType.DMA((PARTS + 1,))],
        compiler_params=pltpu.CompilerParams(vmem_limit_bytes=FIRST_GRANT),
        name="first_step",
    )(final_adjoint, implicit)
    terms, carried = pl.pallas_call(
        first_terms,
        in_specs=[HBM] + [VMEM] * 5,
        out_specs=[VMEM] * 2,
        out_shape=[slots, field],
        scratch_shapes=[planes, rows, pltpu.SemaphoreType.DMA],
        compiler_params=pltpu.CompilerParams(vmem_limit_bytes=24 * MIB),
        name="first_terms",
    )(tile_rows, tile_cols.reshape(1, SLOTS), tile_count.reshape(1, 1), wet, first, tiles)
    for section in range(STEPS - 2, -1, -1):
        gots = exchange(terms, STEPS - 2 - section)
        terms, carried = pl.pallas_call(
            functools.partial(next_kernel, section, len(gots)),
            in_specs=[VMEM] * len(gots) + [HBM] + [VMEM] * 5,
            out_specs=[VMEM] * 2,
            out_shape=[slots, field],
            scratch_shapes=[scratch, planes, scratch, rows, pltpu.SemaphoreType.DMA],
            compiler_params=pltpu.CompilerParams(vmem_limit_bytes=24 * MIB),
            name="next_step",
        )(*gots, tile_rows, wet, carried, implicit, states, tiles)
    gots = exchange(terms, STEPS - 1)
    return pl.pallas_call(
        last_kernel,
        in_specs=[VMEM] * (len(gots) + 3),
        out_specs=VMEM,
        out_shape=field,
        scratch_shapes=[scratch],
        compiler_params=pltpu.CompilerParams(vmem_limit_bytes=24 * MIB),
        name="last_step",
    )(*gots, wet, carried, states)


def solution(mesh):
    in_specs = (
        P(None, None, "col"),
        P(None, None, None, "col"),
        P(None, None, "col"),
        P("col"),
        P("col"),
        P("col"),
        P("col", None, None),
        P("col"),
    )
    out_specs = P(None, None, "col")
    return jax.shard_map(shards, mesh=mesh, in_specs=in_specs, out_specs=out_specs, check_vma=False)
```

```python
import functools
import jax
import jax.numpy as jnp
from jax import lax
from jax.experimental import pallas as pl
from jax.experimental.pallas import tpu as pltpu
from jax.sharding import PartitionSpec as P

STEPS = 3
TRC = 7
LEV = 50
PAD = 56
SLOTS = 30
REACH = 2
KEYS = 2 * REACH + 1
time_step = 0.5
SPAN = 32
INFO = SLOTS
CHUNK = TRC * SPAN
KEY = 64
NONE = -1000.0


def pull_back(states, carried, light):
    phosphate, _, oxygen, plankton, grazers, detritus, nitrate = states
    c_pho, c_dis, c_oxy, c_pla, c_gra, c_det, c_nit = carried
    rp = 1.0 / (0.03 + phosphate)
    rn = 1.0 / (0.5 + nitrate)
    ro = 1.0 / (1.0 + oxygen)
    p2 = plankton * plankton
    rg = 1.0 / (0.1 + p2)
    mix = c_pho - 1.2 * c_oxy + 1.6 * c_nit
    a_growth = 0.1 * c_dis + c_pla - mix
    a_grazing = 0.3 * c_pho - c_pla + 0.7 * c_gra
    a_mortality = 0.1 * c_dis - c_pla + 0.9 * c_det
    a_remineral = mix - c_det
    a_decay = mix - c_dis
    a_loss = c_det - c_gra
    fp = phosphate * rp
    fn = nitrate * rn
    lg = (1.2 * light) * a_growth
    lgp = lg * plankton
    d_pho = lgp * fn * (0.03 * rp * rp)
    d_nit = lgp * fp * (0.5 * rn * rn)
    hol = p2 * rg
    ag = 1.9 * a_grazing
    d_pla = lg * fp * fn + ag * grazers * (0.2 * plankton * rg * rg) + 0.06 * plankton * a_mortality
    d_gra = ag * hol + 0.1 * grazers * a_loss
    ar = 0.05 * a_remineral
    d_det = ar * oxygen * ro
    d_oxy = ar * detritus * (ro * ro)
    d_dis = 0.17 * a_decay
    return [d_pho, d_dis, d_oxy, d_pla, d_gra, d_det, d_nit]


def wet_mask(wet):
    level_ids = lax.broadcasted_iota(jnp.int32, (LEV, 128), 0)
    return (level_ids < wet).astype(jnp.float32)


def product(adj_ref, implicit_ref, arrive=None, parts=1):
    def term(k, acc):
        m = implicit_ref[k]
        return tuple(acc[t] + m * adj_ref[t, pl.ds(k, 1), :] for t in range(TRC))

    acc = tuple(jnp.zeros((LEV, 128), jnp.float32) for _ in range(TRC))
    for part in range(parts):
        if arrive is not None:
            arrive(part)
        acc = lax.fori_loop(part * LEV // parts, (part + 1) * LEV // parts, term, acc, unroll=min(25, LEV // parts))
    return acc


def advance(adj_ref, implicit_ref, wet, carried_ref, planes):
    acc = product(adj_ref, implicit_ref)
    mask = wet_mask(wet)
    for t in range(TRC):
        carried = acc[t] * mask
        planes[pl.ds(t, LEV, stride=8), :] = carried
        carried_ref[t] = carried


def make_terms(planes, tiles_ref, rows, out_ref):
    origin = lax.axis_index("col") * LEV
    for t in range(TRC):
        out_ref[t * SPAN + 24 : (t + 1) * SPAN, :] = jnp.zeros((8, 128), jnp.float32)

    def pick(p):
        row = pl.multiple_of(jnp.clip(rows[p] - origin, 0, LEV - 1) * 8, 8)
        picked = planes[pl.ds(row, 8), :]
        hi = picked.astype(jnp.bfloat16)
        lo = (picked - hi.astype(jnp.float32)).astype(jnp.bfloat16)
        return [hi, lo]

    for p in range(0, SLOTS, 2):
        left = jnp.concatenate(pick(p) + pick(p + 1), axis=0)
        right = jnp.concatenate([tiles_ref[p], tiles_ref[p + 1]], axis=1)
        prod = jnp.dot(left, right, preferred_element_type=jnp.float32)
        out_ref[pl.ds(p, TRC, stride=SPAN), :] = prod[:TRC, :128] + prod[8 : 8 + TRC, :128]
        out_ref[pl.ds(p + 1, TRC, stride=SPAN), :] = prod[16 : 16 + TRC, 128:] + prod[24 : 24 + TRC, 128:]


def first_kernel(final_h, implicit_h, out_ref, implicit, adj, sems):
    span = LEV // PARTS
    copies = [pltpu.make_async_copy(final_h, adj, sems.at[PARTS])]
    for i in range(PARTS):
        part = pl.ds(i * span, span)
        copies.append(pltpu.make_async_copy(implicit_h.at[part], implicit.at[part], sems.at[i]))
    for copy in copies:
        copy.start()
    copies[0].wait()
    acc = product(adj, implicit, lambda i: copies[i + 1].wait(), PARTS)
    for t in range(TRC):
        out_ref[t] = acc[t]


def first_terms(rows_h, cols, count, wet, product_ref, tiles_ref, out_ref, carried_ref, planes, rows, sem):
    copy = pltpu.make_async_copy(rows_h, rows, sem)
    copy.start()
    mask = wet_mask(wet[...])
    for t in range(TRC):
        carried = product_ref[t] * mask
        planes[pl.ds(t, LEV, stride=8), :] = carried
        carried_ref[t] = carried
    place = cols[...] - (lax.axis_index("col") - REACH) * LEV
    key = sum((place >= LEV * j).astype(jnp.int32) for j in range(1, KEYS))
    lane = lax.broadcasted_iota(jnp.int32, (1, SLOTS), 1)
    code = jnp.where(lane < count[...], place + (KEY - LEV) * key, -1).astype(jnp.float32)
    copy.wait()
    make_terms(planes, tiles_ref, rows, out_ref)
    out_ref[INFO : INFO + 1, :] = jnp.full((1, 128), -1.0, jnp.float32)
    for i in range(128 // SPAN):
        out_ref[INFO : INFO + 1, i * SPAN : i * SPAN + SLOTS] = code


def origins(split):
    me = lax.axis_index("col")
    chip = lax.div(me, 2)
    odd = lax.rem(chip, 2)
    if split:
        chips = [chip, chip + 1 - 2 * odd, chip - 1 + 2 * odd]
    else:
        even_edge = chip - odd
        odd_edge = chip - 1 + odd
        away = -(2 ** 20)
        chips = [even_edge, even_edge + 1, jnp.where(odd == 1, away, odd_edge), jnp.where(odd == 1, odd_edge + 1, away)]
    return [2 * c + k for c in chips for k in range(2)]


def receive(chunks, split, take):
    me = lax.axis_index("col")
    lane = lax.broadcasted_iota(jnp.int32, (1, 128), 1)
    level = lax.broadcasted_iota(jnp.int32, (64, 128), 0).astype(jnp.float32)
    bases = [jnp.where(src < -REACH, -100, me - src + REACH) * KEY for src in origins(split)]
    per = 128 // SPAN
    marks = []
    for first in range(0, len(chunks), per):
        number = min(per, len(chunks) - first)
        codes = jnp.full((1, 128), NONE, jnp.float32)
        for i in range(number):
            here = (lane >= i * SPAN) & (lane < (i + 1) * SPAN)
            ref, at = chunks[first + i]
            found = ref[at + INFO : at + INFO + 1, :] - bases[first + i].astype(jnp.float32)
            codes = jnp.where(here, found, codes)
        marks.append((level == codes).astype(jnp.float32).astype(jnp.bfloat16)[:, : number * SPAN])
    marks = jnp.concatenate(marks, axis=1)
    for t in range(TRC):
        data = jnp.concatenate([ref[at + t * SPAN : at + (t + 1) * SPAN, :] for ref, at in chunks], axis=0)
        hi = data.astype(jnp.bfloat16)
        lo = (data - hi.astype(jnp.float32)).astype(jnp.bfloat16)
        both = jnp.dot(marks, jnp.concatenate([hi, lo], axis=1), preferred_element_type=jnp.float32)
        take(t, both[:LEV, :128] + both[:LEV, 128:])


def chunks_of(gots):
    return [(ref, at) for ref in gots for at in range(0, ref.shape[0], CHUNK)]


def local_part(carried_ref, states_ref, section, base):
    level_ids = lax.broadcasted_iota(jnp.int32, (LEV, 128), 0)
    light = jnp.exp(-0.2 * level_ids.astype(jnp.float32))
    carried = [carried_ref[t] for t in range(TRC)]
    bio = pull_back([states_ref[section, t] for t in range(TRC)], carried, light)
    for t in range(TRC):
        base[t] = carried[t] + time_step * bio[t]


def adjoint_into(out_ref, gots, wet_ref, base):
    mask = wet_mask(wet_ref[...])

    def take(t, transport):
        out_ref[t] = mask * (base[t] + transport)

    receive(chunks_of(gots), len(gots) == 2, take)


def next_kernel(section, number, *refs):
    gots, refs = refs[:number], refs[number:]
    (rows_h, wet_ref, carried_in, implicit_ref, states_ref, tiles_ref,
     out_ref, carried_ref, base, planes, adj, rows, sem) = refs
    copy = pltpu.make_async_copy(rows_h, rows, sem)
    copy.start()
    local_part(carried_in, states_ref, section + 1, base)
    adjoint_into(adj, gots, wet_ref, base)
    advance(adj, implicit_ref, wet_ref[...], carried_ref, planes)
    copy.wait()
    make_terms(planes, tiles_ref, rows, out_ref)
    me = lax.axis_index("col")
    core = lax.rem(me, 2)
    own = core if number == 2 else 2 * lax.rem(lax.div(me, 2), 2) + core
    out_ref[INFO : INFO + 1, :] = gots[0][pl.ds(own * CHUNK + INFO, 1), :]


def last_kernel(*refs):
    gots, (wet_ref, carried_in, states_ref, out_ref, base) = refs[:-5], refs[-5:]
    local_part(carried_in, states_ref, 0, base)
    adjoint_into(out_ref, gots, wet_ref, base)


VMEM = pl.BlockSpec(memory_space=pltpu.VMEM)
HBM = pl.BlockSpec(memory_space=pltpu.HBM)
f32 = jnp.float32
PARTS = 5
SWAP_STEP = 1
MIB = 1024 * 1024
FIRST_GRANT = 56255054


def shards(final_adjoint, states, implicit, wet_levels, tile_rows, tile_cols, tiles, tile_count):
    devices = lax.axis_size("col")
    inside = [[2 * c, 2 * c + 1] for c in range(devices // 2)]
    across = [[2 * c, 2 * c + 2] for c in range(0, devices // 2, 2)]
    across += [[2 * c + 1, (2 * c + 3) % devices] for c in range(1, devices // 2, 2)]
    swaps = [pair for a, b in across[:-1] for pair in ((a, b), (b, a))]
    slots = jax.ShapeDtypeStruct((CHUNK, 128), f32)
    field = jax.ShapeDtypeStruct((TRC, LEV, 128), f32)
    scratch = pltpu.VMEM((TRC, LEV, 128), f32)
    planes = pltpu.VMEM((PAD * 8, 128), f32)
    rows = pltpu.SMEM((SLOTS,), jnp.int32)
    wet = wet_levels.reshape(1, 128)

    def gather(x, groups):
        return lax.all_gather(x, "col", axis_index_groups=groups, tiled=True)

    me = lax.axis_index("col")
    second_of_pair = lax.rem(lax.div(me, 2) + me, 2) == 1

    def exchange(terms, step):
        own = gather(terms, inside)
        if step == SWAP_STEP:
            met = lax.ppermute(own, "col", swaps)
        else:
            both = gather(own, across)
            met = jnp.where(second_of_pair, both[: 2 * CHUNK], both[2 * CHUNK :])
        return own, gather(met, inside)

    first = pl.pallas_call(
        first_kernel,
        in_specs=[HBM] * 2,
        out_specs=VMEM,
        out_shape=field,
        scratch_shapes=[pltpu.VMEM(implicit.shape, f32), scratch, pltpu.SemaphoreType.DMA((PARTS + 1,))],
        compiler_params=pltpu.CompilerParams(vmem_limit_bytes=FIRST_GRANT),
        name="first_step",
    )(final_adjoint, implicit)
    terms, carried = pl.pallas_call(
        first_terms,
        in_specs=[HBM] + [VMEM] * 5,
        out_specs=[VMEM] * 2,
        out_shape=[slots, field],
        scratch_shapes=[planes, rows, pltpu.SemaphoreType.DMA],
        compiler_params=pltpu.CompilerParams(vmem_limit_bytes=24 * MIB),
        name="first_terms",
    )(tile_rows, tile_cols.reshape(1, SLOTS), tile_count.reshape(1, 1), wet, first, tiles)
    for section in range(STEPS - 2, -1, -1):
        gots = exchange(terms, STEPS - 2 - section)
        terms, carried = pl.pallas_call(
            functools.partial(next_kernel, section, len(gots)),
            in_specs=[VMEM] * len(gots) + [HBM] + [VMEM] * 5,
            out_specs=[VMEM] * 2,
            out_shape=[slots, field],
            scratch_shapes=[scratch, planes, scratch, rows, pltpu.SemaphoreType.DMA],
            compiler_params=pltpu.CompilerParams(vmem_limit_bytes=24 * MIB),
            name="next_step",
        )(*gots, tile_rows, wet, carried, implicit, states, tiles)
    gots = exchange(terms, STEPS - 1)
    return pl.pallas_call(
        last_kernel,
        in_specs=[VMEM] * (len(gots) + 3),
        out_specs=VMEM,
        out_shape=field,
        scratch_shapes=[scratch],
        compiler_params=pltpu.CompilerParams(vmem_limit_bytes=24 * MIB),
        name="last_step",
    )(*gots, wet, carried, states)


def solution(mesh):
    in_specs = (
        P(None, None, "col"),
        P(None, None, None, "col"),
        P(None, None, "col"),
        P("col"),
        P("col"),
        P("col"),
        P("col", None, None),
        P("col"),
    )
    out_specs = P(None, None, "col")
    return jax.shard_map(shards, mesh=mesh, in_specs=in_specs, out_specs=out_specs, check_vma=False)
```

```python
import functools
import jax
import jax.numpy as jnp
from jax import lax
from jax.experimental import pallas as pl
from jax.experimental.pallas import tpu as pltpu
from jax.sharding import PartitionSpec as P

STEPS = 3
TRC = 7
LEV = 50
PAD = 56
SLOTS = 30
REACH = 2
KEYS = 2 * REACH + 1
time_step = 0.5
SPAN = 32
INFO = SLOTS
CHUNK = TRC * SPAN
KEY = 64
NONE = -1000.0


def pull_back(states, carried, light):
    phosphate, _, oxygen, plankton, grazers, detritus, nitrate = states
    c_pho, c_dis, c_oxy, c_pla, c_gra, c_det, c_nit = carried
    rp = 1.0 / (0.03 + phosphate)
    rn = 1.0 / (0.5 + nitrate)
    ro = 1.0 / (1.0 + oxygen)
    p2 = plankton * plankton
    rg = 1.0 / (0.1 + p2)
    mix = c_pho - 1.2 * c_oxy + 1.6 * c_nit
    a_growth = 0.1 * c_dis + c_pla - mix
    a_grazing = 0.3 * c_pho - c_pla + 0.7 * c_gra
    a_mortality = 0.1 * c_dis - c_pla + 0.9 * c_det
    a_remineral = mix - c_det
    a_decay = mix - c_dis
    a_loss = c_det - c_gra
    fp = phosphate * rp
    fn = nitrate * rn
    lg = (1.2 * light) * a_growth
    lgp = lg * plankton
    d_pho = lgp * fn * (0.03 * rp * rp)
    d_nit = lgp * fp * (0.5 * rn * rn)
    hol = p2 * rg
    ag = 1.9 * a_grazing
    d_pla = lg * fp * fn + ag * grazers * (0.2 * plankton * rg * rg) + 0.06 * plankton * a_mortality
    d_gra = ag * hol + 0.1 * grazers * a_loss
    ar = 0.05 * a_remineral
    d_det = ar * oxygen * ro
    d_oxy = ar * detritus * (ro * ro)
    d_dis = 0.17 * a_decay
    return [d_pho, d_dis, d_oxy, d_pla, d_gra, d_det, d_nit]


def wet_mask(wet):
    level_ids = lax.broadcasted_iota(jnp.int32, (LEV, 128), 0)
    return (level_ids < wet).astype(jnp.float32)


def product(adj_ref, implicit_ref, arrive=None, parts=1, lower=None):
    def term(k, acc):
        m = implicit_ref[k]
        return tuple(acc[t] + m * adj_ref[t, pl.ds(k, 1), :] for t in range(TRC))

    def lower_term(k, acc):
        m = lower[k]
        return tuple(acc[t] + m * adj_ref[t, pl.ds(k + LEV // 2, 1), :] for t in range(TRC))

    acc = tuple(jnp.zeros((LEV, 128), jnp.float32) for _ in range(TRC))
    if lower is not None:
        acc = lax.fori_loop(0, LEV // 2, term, acc, unroll=LEV // 2)
        return lax.fori_loop(0, LEV // 2, lower_term, acc, unroll=LEV // 2)
    for part in range(parts):
        if arrive is not None:
            arrive(part)
        acc = lax.fori_loop(part * LEV // parts, (part + 1) * LEV // parts, term, acc, unroll=min(25, LEV // parts))
    return acc


def carry(acc, wet, states_ref, base_ref, planes, arrive):
    mask = wet_mask(wet)
    level_ids = lax.broadcasted_iota(jnp.int32, (LEV, 128), 0)
    light = jnp.exp(-0.2 * level_ids.astype(jnp.float32))
    carried = [acc[t] * mask for t in range(TRC)]
    for t in range(TRC):
        planes[pl.ds(t, LEV, stride=8), :] = carried[t]
    arrive()
    bio = pull_back([states_ref[t] for t in range(TRC)], carried, light)
    for t in range(TRC):
        base_ref[t] = carried[t] + time_step * bio[t]


def make_terms(planes, tiles_ref, rows, sums, out_ref):
    origin = lax.axis_index("col") * LEV
    for t in range(TRC):
        sums[t * SPAN + 24 : (t + 1) * SPAN, :] = jnp.zeros((8, 128), jnp.float32)

    def pick(p):
        row = pl.multiple_of(jnp.clip(rows[p] - origin, 0, LEV - 1) * 8, 8)
        picked = planes[pl.ds(row, 8), :]
        hi = picked.astype(jnp.bfloat16)
        lo = (picked - hi.astype(jnp.float32)).astype(jnp.bfloat16)
        return [hi, lo]

    for p in range(0, SLOTS, 2):
        left = jnp.concatenate(pick(p) + pick(p + 1), axis=0)
        right = jnp.concatenate([tiles_ref[p], tiles_ref[p + 1]], axis=1)
        prod = jnp.dot(left, right, preferred_element_type=jnp.float32)
        sums[pl.ds(p, 8, stride=SPAN), :] = prod[:8, :128] + prod[8:16, :128]
        sums[pl.ds(p + 1, 8, stride=SPAN), :] = prod[16:24, 128:] + prod[24:, 128:]
    out_ref[...] = sums[:CHUNK, :]


def fetch(implicit_h, implicit, sems):
    span = LEV // PARTS
    copies = []
    for i in range(PARTS):
        part = pl.ds(i * span, span)
        copies.append(pltpu.make_async_copy(implicit_h.at[part], implicit.at[part], sems.at[i]))
        copies[-1].start()
    return lambda i: copies[i].wait()


def first_kernel(final_h, implicit_h, out_ref, implicit, adj, sems):
    copy = pltpu.make_async_copy(final_h, adj, sems.at[PARTS])
    copy.start()
    arrive = fetch(implicit_h, implicit, sems)
    copy.wait()
    acc = product(adj, implicit, arrive, PARTS)
    for t in range(TRC):
        out_ref[t] = acc[t]


def first_terms(rows_h, cols, count, wet, product_ref, states_h, implicit_h, tiles_ref,
                out_ref, base_ref, upper, lower, planes, rows, states, sums, sems):
    halves = []
    for i, half in enumerate((upper, lower)):
        part = implicit_h.at[pl.ds(i * (LEV // 2), LEV // 2)]
        halves.append(pltpu.make_async_copy(part, half, sems.at[2 + i]))
    copy = pltpu.make_async_copy(rows_h, rows, sems.at[0])
    copy.start()
    for half in halves:
        half.start()
    state_copy = pltpu.make_async_copy(states_h.at[STEPS - 1], states, sems.at[1])
    state_copy.start()
    carry([product_ref[t] for t in range(TRC)], wet[...], states, base_ref, planes, state_copy.wait)
    place = cols[...] - (lax.axis_index("col") - REACH) * LEV
    key = sum((place >= LEV * j).astype(jnp.int32) for j in range(1, KEYS))
    lane = lax.broadcasted_iota(jnp.int32, (1, SLOTS), 1)
    code = jnp.where(lane < count[...], place + (KEY - LEV) * key, -1).astype(jnp.float32)
    copy.wait()
    make_terms(planes, tiles_ref, rows, sums, out_ref)
    out_ref[INFO : INFO + 1, :] = jnp.full((1, 128), -1.0, jnp.float32)
    for i in range(128 // SPAN):
        out_ref[INFO : INFO + 1, i * SPAN : i * SPAN + SLOTS] = code
    for half in halves:
        half.wait()


def origins():
    chip = lax.div(lax.axis_index("col"), 2)
    odd = lax.rem(chip, 2)
    return [2 * c + k for c in (chip, chip + 1 - 2 * odd, chip - 1 + 2 * odd) for k in range(2)]


def receive(chunks, take):
    me = lax.axis_index("col")
    lane = lax.broadcasted_iota(jnp.int32, (1, 128), 1)
    level = lax.broadcasted_iota(jnp.int32, (64, 128), 0).astype(jnp.float32)
    bases = [(me - src + REACH) * KEY for src in origins()]
    per = 128 // SPAN
    marks = []
    for first in range(0, len(chunks), per):
        number = min(per, len(chunks) - first)
        codes = jnp.full((1, 128), NONE, jnp.float32)
        for i in range(number):
            here = (lane >= i * SPAN) & (lane < (i + 1) * SPAN)
            ref, at = chunks[first + i]
            found = ref[at + INFO : at + INFO + 1, :] - bases[first + i].astype(jnp.float32)
            codes = jnp.where(here, found, codes)
        marks.append((level == codes).astype(jnp.float32).astype(jnp.bfloat16)[:, : number * SPAN])
    marks = jnp.concatenate(marks, axis=1)
    for t in range(TRC):
        data = jnp.concatenate([ref[at + t * SPAN : at + (t + 1) * SPAN, :] for ref, at in chunks], axis=0)
        hi = data.astype(jnp.bfloat16)
        lo = (data - hi.astype(jnp.float32)).astype(jnp.bfloat16)
        both = jnp.dot(marks, jnp.concatenate([hi, lo], axis=1), preferred_element_type=jnp.float32)
        take(t, both[:LEV, :128] + both[:LEV, 128:])


def chunks_of(gots):
    return [(ref, at) for ref in gots for at in range(0, ref.shape[0], CHUNK)]


def adjoint_into(out_ref, gots, wet_ref, base):
    mask = wet_mask(wet_ref[...])

    def take(t, transport):
        out_ref[t] = mask * (base[t] + transport)

    receive(chunks_of(gots), take)


def next_kernel(section, own_ref, got_ref, rows_h, wet_ref, base_in, upper, lower, states_h, tiles_h,
                out_ref, base_ref, planes, adj, rows, states, tiles_ref, sums, sems):
    tile_copy = pltpu.make_async_copy(tiles_h, tiles_ref, sems.at[0])
    tile_copy.start()
    copy = pltpu.make_async_copy(rows_h, rows, sems.at[1])
    copy.start()
    state_copy = pltpu.make_async_copy(states_h.at[section], states, sems.at[2])
    state_copy.start()
    adjoint_into(adj, (own_ref, got_ref), wet_ref, base_in)
    carry(product(adj, upper, lower=lower), wet_ref[...], states, base_ref, planes, state_copy.wait)
    copy.wait()
    tile_copy.wait()
    make_terms(planes, tiles_ref, rows, sums, out_ref)
    core = lax.rem(lax.axis_index("col"), 2)
    out_ref[INFO : INFO + 1, :] = own_ref[pl.ds(core * CHUNK + INFO, 1), :]


def last_kernel(own_ref, got_ref, wet_ref, base_in, out_ref):
    adjoint_into(out_ref, (own_ref, got_ref), wet_ref, base_in)


VMEM = pl.BlockSpec(memory_space=pltpu.VMEM)
HBM = pl.BlockSpec(memory_space=pltpu.HBM)
f32 = jnp.float32
PARTS = 5
MIB = 1024 * 1024
FIRST_GRANT = 56255054
TERMS_GRANT = 50 * MIB
NEXT_GRANT = int(50.2 * MIB)


def shards(final_adjoint, states, implicit, wet_levels, tile_rows, tile_cols, tiles, tile_count):
    devices = lax.axis_size("col")
    inside = [[2 * c, 2 * c + 1] for c in range(devices // 2)]
    across = [[2 * c, 2 * c + 2] for c in range(0, devices // 2, 2)]
    across += [[2 * c + 1, (2 * c + 3) % devices] for c in range(1, devices // 2, 2)]
    slots = jax.ShapeDtypeStruct((CHUNK, 128), f32)
    field = jax.ShapeDtypeStruct((TRC, LEV, 128), f32)
    scratch = pltpu.VMEM((TRC, LEV, 128), f32)
    planes = pltpu.VMEM((PAD * 8, 128), f32)
    sums = pltpu.VMEM((8 * SPAN, 128), f32)
    matrix = pltpu.VMEM(implicit.shape, f32)
    rows = pltpu.SMEM((SLOTS,), jnp.int32)
    wet = wet_levels.reshape(1, 128)

    def gather(x, groups):
        return lax.all_gather(x, "col", axis_index_groups=groups, tiled=True)

    me = lax.axis_index("col")
    second_of_pair = lax.rem(lax.div(me, 2) + me, 2) == 1

    alone = (me == across[-1][0]) | (me == across[-1][1])

    def exchange(terms):
        own = gather(terms, inside)

        def meet(x):
            both = gather(x, across)
            return jnp.where(second_of_pair, both[: 2 * CHUNK], both[2 * CHUNK :])

        met = lax.cond(alone, jnp.zeros_like, meet, own)
        return own, gather(met, inside)

    first = pl.pallas_call(
        first_kernel,
        in_specs=[HBM] * 2,
        out_specs=VMEM,
        out_shape=field,
        scratch_shapes=[matrix, scratch, pltpu.SemaphoreType.DMA((PARTS + 1,))],
        compiler_params=pltpu.CompilerParams(vmem_limit_bytes=FIRST_GRANT),
        name="first_step",
    )(final_adjoint, implicit)
    half = jax.ShapeDtypeStruct((LEV // 2, LEV, 128), f32)
    terms, base, upper, lower = pl.pallas_call(
        first_terms,
        in_specs=[HBM] + [VMEM] * 4 + [HBM, HBM, VMEM],
        out_specs=[VMEM] * 4,
        out_shape=[slots, field, half, half],
        scratch_shapes=[planes, rows, scratch, sums, pltpu.SemaphoreType.DMA((4,))],
        compiler_params=pltpu.CompilerParams(vmem_limit_bytes=TERMS_GRANT),
        name="first_terms",
    )(tile_rows, tile_cols.reshape(1, SLOTS), tile_count.reshape(1, 1), wet, first, states, implicit, tiles)
    for section in range(STEPS - 2, -1, -1):
        own, got = exchange(terms)
        terms, base = pl.pallas_call(
            functools.partial(next_kernel, section),
            in_specs=[VMEM] * 2 + [HBM] + [VMEM] * 4 + [HBM, HBM],
            out_specs=[VMEM] * 2,
            out_shape=[slots, field],
            scratch_shapes=[
                planes,
                scratch,
                rows,
                scratch,
                pltpu.VMEM(tiles.shape, tiles.dtype),
                sums,
                pltpu.SemaphoreType.DMA((3,)),
            ],
            compiler_params=pltpu.CompilerParams(vmem_limit_bytes=NEXT_GRANT),
            name="next_step",
        )(own, got, tile_rows, wet, base, upper, lower, states, tiles)
    own, got = exchange(terms)
    return pl.pallas_call(
        last_kernel,
        in_specs=[VMEM] * 4,
        out_specs=VMEM,
        out_shape=field,
        compiler_params=pltpu.CompilerParams(vmem_limit_bytes=24 * MIB),
        name="last_step",
    )(own, got, wet, base)


def solution(mesh):
    in_specs = (
        P(None, None, "col"),
        P(None, None, None, "col"),
        P(None, None, "col"),
        P("col"),
        P("col"),
        P("col"),
        P("col", None, None),
        P("col"),
    )
    out_specs = P(None, None, "col")
    return jax.shard_map(shards, mesh=mesh, in_specs=in_specs, out_specs=out_specs, check_vma=False)
```

```python
import functools
import jax
import jax.numpy as jnp
from jax import lax
from jax.experimental import pallas as pl
from jax.experimental.pallas import tpu as pltpu
from jax.sharding import PartitionSpec as P

STEPS = 3
TRC = 7
LEV = 50
PAD = 56
SLOTS = 30
REACH = 2
KEYS = 2 * REACH + 1
time_step = 0.5
SPAN = 32
INFO = SLOTS
KEPT = 10
CHUNK = TRC * SPAN
KEY = 64
NONE = -1000.0


def pull_back(states, carried, light):
    phosphate, _, oxygen, plankton, grazers, detritus, nitrate = states
    c_pho, c_dis, c_oxy, c_pla, c_gra, c_det, c_nit = carried
    rp = 1.0 / (0.03 + phosphate)
    rn = 1.0 / (0.5 + nitrate)
    ro = 1.0 / (1.0 + oxygen)
    p2 = plankton * plankton
    rg = 1.0 / (0.1 + p2)
    mix = c_pho - 1.2 * c_oxy + 1.6 * c_nit
    a_growth = 0.1 * c_dis + c_pla - mix
    a_grazing = 0.3 * c_pho - c_pla + 0.7 * c_gra
    a_mortality = 0.1 * c_dis - c_pla + 0.9 * c_det
    a_remineral = mix - c_det
    a_decay = mix - c_dis
    a_loss = c_det - c_gra
    fp = phosphate * rp
    fn = nitrate * rn
    lg = (1.2 * light) * a_growth
    lgp = lg * plankton
    d_pho = lgp * fn * (0.03 * rp * rp)
    d_nit = lgp * fp * (0.5 * rn * rn)
    hol = p2 * rg
    ag = 1.9 * a_grazing
    d_pla = lg * fp * fn + ag * grazers * (0.2 * plankton * rg * rg) + 0.06 * plankton * a_mortality
    d_gra = ag * hol + 0.1 * grazers * a_loss
    ar = 0.05 * a_remineral
    d_det = ar * oxygen * ro
    d_oxy = ar * detritus * (ro * ro)
    d_dis = 0.17 * a_decay
    return [d_pho, d_dis, d_oxy, d_pla, d_gra, d_det, d_nit]


def wet_mask(wet):
    level_ids = lax.broadcasted_iota(jnp.int32, (LEV, 128), 0)
    return (level_ids < wet).astype(jnp.float32)


def product(adj_ref, implicit_ref, arrive=None, parts=1, lower=None):
    def term(k, acc):
        m = implicit_ref[k]
        return tuple(acc[t] + m * adj_ref[t, pl.ds(k, 1), :] for t in range(TRC))

    def lower_term(k, acc):
        m = lower[k]
        return tuple(acc[t] + m * adj_ref[t, pl.ds(k + LEV // 2, 1), :] for t in range(TRC))

    acc = tuple(jnp.zeros((LEV, 128), jnp.float32) for _ in range(TRC))
    if lower is not None:
        acc = lax.fori_loop(0, LEV // 2, term, acc, unroll=LEV // 2)
        return lax.fori_loop(0, LEV // 2, lower_term, acc, unroll=LEV // 2)
    for part in range(parts):
        if arrive is not None:
            arrive(part)
        acc = lax.fori_loop(part * LEV // parts, (part + 1) * LEV // parts, term, acc, unroll=min(25, LEV // parts))
    return acc


def carry(acc, wet, states_ref, base_ref, planes, arrive):
    mask = wet_mask(wet)
    level_ids = lax.broadcasted_iota(jnp.int32, (LEV, 128), 0)
    light = jnp.exp(-0.2 * level_ids.astype(jnp.float32))
    carried = [acc[t] * mask for t in range(TRC)]
    for t in range(TRC):
        planes[pl.ds(t, LEV, stride=8), :] = carried[t]
    arrive()
    bio = pull_back([states_ref[t] for t in range(TRC)], carried, light)
    for t in range(TRC):
        base_ref[t] = carried[t] + time_step * bio[t]


def make_terms(planes, tile, rows, sums, out_ref):
    origin = lax.axis_index("col") * LEV
    for t in range(TRC):
        sums[t * SPAN + 24 : (t + 1) * SPAN, :] = jnp.zeros((8, 128), jnp.float32)

    def pick(p):
        row = pl.multiple_of(jnp.clip(rows[p] - origin, 0, LEV - 1) * 8, 8)
        picked = planes[pl.ds(row, 8), :]
        hi = picked.astype(jnp.bfloat16)
        lo = (picked - hi.astype(jnp.float32)).astype(jnp.bfloat16)
        return [hi, lo]

    for p in range(0, SLOTS, 2):
        left = jnp.concatenate(pick(p) + pick(p + 1), axis=0)
        right = jnp.concatenate([tile(p), tile(p + 1)], axis=1)
        prod = jnp.dot(left, right, preferred_element_type=jnp.float32)
        sums[pl.ds(p, 8, stride=SPAN), :] = prod[:8, :128] + prod[8:16, :128]
        sums[pl.ds(p + 1, 8, stride=SPAN), :] = prod[16:24, 128:] + prod[24:, 128:]
    out_ref[...] = sums[:CHUNK, :]


def fetch(implicit_h, implicit, sems):
    span = LEV // PARTS
    copies = []
    for i in range(PARTS):
        part = pl.ds(i * span, span)
        copies.append(pltpu.make_async_copy(implicit_h.at[part], implicit.at[part], sems.at[i]))
        copies[-1].start()
    return lambda i: copies[i].wait()


def first_kernel(final_h, implicit_h, out_ref, implicit, adj, sems):
    copy = pltpu.make_async_copy(final_h, adj, sems.at[PARTS])
    copy.start()
    arrive = fetch(implicit_h, implicit, sems)
    copy.wait()
    acc = product(adj, implicit, arrive, PARTS)
    for t in range(TRC):
        out_ref[t] = acc[t]


def first_terms(rows_h, cols, count, wet, product_ref, states_h, implicit_h, tiles_ref,
                out_ref, base_ref, upper, lower, kept, planes, rows, states, sums, sems):
    halves = []
    for i, half in enumerate((upper, lower)):
        part = implicit_h.at[pl.ds(i * (LEV // 2), LEV // 2)]
        halves.append(pltpu.make_async_copy(part, half, sems.at[2 + i]))
    halves.append(pltpu.make_async_copy(tiles_ref.at[pl.ds(0, KEPT)], kept, sems.at[4]))
    copy = pltpu.make_async_copy(rows_h, rows, sems.at[0])
    copy.start()
    for half in halves:
        half.start()
    state_copy = pltpu.make_async_copy(states_h.at[STEPS - 1], states, sems.at[1])
    state_copy.start()
    carry([product_ref[t] for t in range(TRC)], wet[...], states, base_ref, planes, state_copy.wait)
    place = cols[...] - (lax.axis_index("col") - REACH) * LEV
    key = sum((place >= LEV * j).astype(jnp.int32) for j in range(1, KEYS))
    lane = lax.broadcasted_iota(jnp.int32, (1, SLOTS), 1)
    code = jnp.where(lane < count[...], place + (KEY - LEV) * key, -1).astype(jnp.float32)
    copy.wait()
    make_terms(planes, lambda p: tiles_ref[p], rows, sums, out_ref)
    out_ref[INFO : INFO + 1, :] = jnp.full((1, 128), -1.0, jnp.float32)
    for i in range(128 // SPAN):
        out_ref[INFO : INFO + 1, i * SPAN : i * SPAN + SLOTS] = code
    for half in halves:
        half.wait()


def origins():
    chip = lax.div(lax.axis_index("col"), 2)
    odd = lax.rem(chip, 2)
    return [2 * c + k for c in (chip, chip + 1 - 2 * odd, chip - 1 + 2 * odd) for k in range(2)]


def receive(chunks, take):
    me = lax.axis_index("col")
    lane = lax.broadcasted_iota(jnp.int32, (1, 128), 1)
    level = lax.broadcasted_iota(jnp.int32, (64, 128), 0).astype(jnp.float32)
    bases = [(me - src + REACH) * KEY for src in origins()]
    per = 128 // SPAN
    marks = []
    for first in range(0, len(chunks), per):
        number = min(per, len(chunks) - first)
        codes = jnp.full((1, 128), NONE, jnp.float32)
        for i in range(number):
            here = (lane >= i * SPAN) & (lane < (i + 1) * SPAN)
            ref, at = chunks[first + i]
            found = ref[at + INFO : at + INFO + 1, :] - bases[first + i].astype(jnp.float32)
            codes = jnp.where(here, found, codes)
        marks.append((level == codes).astype(jnp.float32).astype(jnp.bfloat16)[:, : number * SPAN])
    marks = jnp.concatenate(marks, axis=1)
    for t in range(TRC):
        data = jnp.concatenate([ref[at + t * SPAN : at + (t + 1) * SPAN, :] for ref, at in chunks], axis=0)
        hi = data.astype(jnp.bfloat16)
        lo = (data - hi.astype(jnp.float32)).astype(jnp.bfloat16)
        both = jnp.dot(marks, jnp.concatenate([hi, lo], axis=1), preferred_element_type=jnp.float32)
        take(t, both[:LEV, :128] + both[:LEV, 128:])


def chunks_of(gots):
    return [(ref, at) for ref in gots for at in range(0, ref.shape[0], CHUNK)]


def adjoint_into(out_ref, gots, wet_ref, base):
    mask = wet_mask(wet_ref[...])

    def take(t, transport):
        out_ref[t] = mask * (base[t] + transport)

    receive(chunks_of(gots), take)


def next_kernel(section, own_ref, got_ref, rows_h, wet_ref, base_in, upper, lower, kept, states_h, tiles_h,
                out_ref, base_ref, planes, adj, rows, states, tiles_ref, sums, sems):
    tile_copy = pltpu.make_async_copy(tiles_h.at[pl.ds(KEPT, SLOTS - KEPT)], tiles_ref, sems.at[0])
    tile_copy.start()
    copy = pltpu.make_async_copy(rows_h, rows, sems.at[1])
    copy.start()
    state_copy = pltpu.make_async_copy(states_h.at[section], states, sems.at[2])
    state_copy.start()
    adjoint_into(adj, (own_ref, got_ref), wet_ref, base_in)
    carry(product(adj, upper, lower=lower), wet_ref[...], states, base_ref, planes, state_copy.wait)
    copy.wait()
    tile_copy.wait()
    make_terms(planes, lambda p: kept[p] if p < KEPT else tiles_ref[p - KEPT], rows, sums, out_ref)
    core = lax.rem(lax.axis_index("col"), 2)
    out_ref[INFO : INFO + 1, :] = own_ref[pl.ds(core * CHUNK + INFO, 1), :]


def last_kernel(own_ref, got_ref, wet_ref, base_in, out_ref):
    adjoint_into(out_ref, (own_ref, got_ref), wet_ref, base_in)


VMEM = pl.BlockSpec(memory_space=pltpu.VMEM)
HBM = pl.BlockSpec(memory_space=pltpu.HBM)
f32 = jnp.float32
PARTS = 5
MIB = 1024 * 1024
FIRST_GRANT = 56255054
TERMS_GRANT = 50 * MIB
NEXT_GRANT = int(50.2 * MIB)


def shards(final_adjoint, states, implicit, wet_levels, tile_rows, tile_cols, tiles, tile_count):
    devices = lax.axis_size("col")
    inside = [[2 * c, 2 * c + 1] for c in range(devices // 2)]
    across = [[2 * c, 2 * c + 2] for c in range(0, devices // 2, 2)]
    across += [[2 * c + 1, (2 * c + 3) % devices] for c in range(1, devices // 2, 2)]
    slots = jax.ShapeDtypeStruct((CHUNK, 128), f32)
    field = jax.ShapeDtypeStruct((TRC, LEV, 128), f32)
    scratch = pltpu.VMEM((TRC, LEV, 128), f32)
    planes = pltpu.VMEM((PAD * 8, 128), f32)
    sums = pltpu.VMEM((8 * SPAN, 128), f32)
    matrix = pltpu.VMEM(implicit.shape, f32)
    rows = pltpu.SMEM((SLOTS,), jnp.int32)
    wet = wet_levels.reshape(1, 128)

    def gather(x, groups):
        return lax.all_gather(x, "col", axis_index_groups=groups, tiled=True)

    me = lax.axis_index("col")
    second_of_pair = lax.rem(lax.div(me, 2) + me, 2) == 1

    alone = (me == across[-1][0]) | (me == across[-1][1])

    def exchange(terms):
        own = gather(terms, inside)

        def meet(x):
            both = gather(x, across)
            return jnp.where(second_of_pair, both[: 2 * CHUNK], both[2 * CHUNK :])

        met = lax.cond(alone, jnp.zeros_like, meet, own)
        return own, gather(met, inside)

    first = pl.pallas_call(
        first_kernel,
        in_specs=[HBM] * 2,
        out_specs=VMEM,
        out_shape=field,
        scratch_shapes=[matrix, scratch, pltpu.SemaphoreType.DMA((PARTS + 1,))],
        compiler_params=pltpu.CompilerParams(vmem_limit_bytes=FIRST_GRANT),
        name="first_step",
    )(final_adjoint, implicit)
    half = jax.ShapeDtypeStruct((LEV // 2, LEV, 128), f32)
    terms, base, upper, lower, kept = pl.pallas_call(
        first_terms,
        in_specs=[HBM] + [VMEM] * 4 + [HBM, HBM, VMEM],
        out_specs=[VMEM] * 5,
        out_shape=[slots, field, half, half, jax.ShapeDtypeStruct((KEPT, 128, 128), tiles.dtype)],
        scratch_shapes=[planes, rows, scratch, sums, pltpu.SemaphoreType.DMA((5,))],
        compiler_params=pltpu.CompilerParams(vmem_limit_bytes=TERMS_GRANT),
        name="first_terms",
    )(tile_rows, tile_cols.reshape(1, SLOTS), tile_count.reshape(1, 1), wet, first, states, implicit, tiles)
    for section in range(STEPS - 2, -1, -1):
        own, got = exchange(terms)
        terms, base = pl.pallas_call(
            functools.partial(next_kernel, section),
            in_specs=[VMEM] * 2 + [HBM] + [VMEM] * 5 + [HBM, HBM],
            out_specs=[VMEM] * 2,
            out_shape=[slots, field],
            scratch_shapes=[
                planes,
                scratch,
                rows,
                scratch,
                pltpu.VMEM((SLOTS - KEPT, 128, 128), tiles.dtype),
                sums,
                pltpu.SemaphoreType.DMA((3,)),
            ],
            compiler_params=pltpu.CompilerParams(vmem_limit_bytes=NEXT_GRANT),
            name="next_step",
        )(own, got, tile_rows, wet, base, upper, lower, kept, states, tiles)
    own, got = exchange(terms)
    return pl.pallas_call(
        last_kernel,
        in_specs=[VMEM] * 4,
        out_specs=VMEM,
        out_shape=field,
        compiler_params=pltpu.CompilerParams(vmem_limit_bytes=24 * MIB),
        name="last_step",
    )(own, got, wet, base)


def solution(mesh):
    in_specs = (
        P(None, None, "col"),
        P(None, None, None, "col"),
        P(None, None, "col"),
        P("col"),
        P("col"),
        P("col"),
        P("col", None, None),
        P("col"),
    )
    out_specs = P(None, None, "col")
    return jax.shard_map(shards, mesh=mesh, in_specs=in_specs, out_specs=out_specs, check_vma=False)
```
